32 devices in a mesh: section: 4 (over y, x), seq: 8 (over z, core).
Axes of the slice: x: 2, y: 2, z: 4, core: 2. Of those that a mesh axis runs over, the one named last changes fastest.
Arguments:
- section_inputs: bfloat16 [4, 2, 4096, 256], P('section', None, 'seq'), may hold values from -6 to 6
- cotangent: bfloat16 [2, 4096, 256], P(None, 'seq'), may hold values from -6 to 6
- conv_weight: bfloat16 [4, 2, 3, 256, 512], P('section'), may hold values from -0.21875 to 0.21875
- out_weight: bfloat16 [4, 2, 256, 256], P('section'), may hold values from -0.375 to 0.375
Outputs:
- input_grads: float32 [4, 2, 4096, 256], P('section', None, 'seq')
- conv_grads: float32 [4, 2, 768, 512], P('section', None, 'seq')
- out_grads: float32 [4, 2, 256, 256], P('section', None, 'seq')
The draws below stay inside these ranges and needn't reach their ends.
All inputs are finite; a program needn't handle non-finite values.
Results may differ from the reference program's by a relative error of at most 0.019.
Values may be sent and summed in bfloat16 or wider, within the bound.
A program may use at most 128 MiB of HBM per device.

```python
import math
import jax
import jax.numpy as jnp
from jax import lax

C = 256
LAYERS = 2
MICRO = 2
SECTIONS = 4
WINDOW = 4096
NEAR = 128
FAR = 1024


def shard_levels(rng, dims, split, low, top_value):
    factor_of, own = 1.0, jax.random.fold_in(rng, 6)
    for dim, shards_of in split:
        heights = jnp.exp(jax.random.uniform(jax.random.fold_in(own, dim), (shards_of,), jnp.float32, low / len(split), top_value / len(split)))
        factor_of = factor_of * jnp.repeat(heights, dims[dim] // shards_of).reshape([-1 if axis == dim else 1 for axis in range(len(dims))])
    return factor_of


def centred(rng, dims, scale, limit, cuts=(), held_as=jnp.bfloat16):
    loudness = shard_levels(rng, dims, cuts, -0.22, 0.18) if cuts else 1.0
    entries = jax.random.normal(rng, dims, jnp.float32) * scale * loudness
    return jnp.minimum(jnp.maximum(entries, -limit), limit).astype(held_as)


def setup_inputs(seed: int = 0) -> dict:
    keys = jax.random.split(jax.random.key(seed), 5)
    return {
        "section_inputs": centred(keys[0], (SECTIONS, MICRO, WINDOW, C), 1.0, 6.0, ((0, 4), (2, 8))),
        "cotangent": centred(keys[1], (MICRO, WINDOW, C), 1.0, 6.0, ((1, 8),)),
        "conv_weight": centred(keys[2], (SECTIONS, LAYERS, 3, C, 2 * C), (3 * C) ** -0.5, 0.21875, ((0, 4),)),
        "out_weight": centred(keys[3], (SECTIONS, LAYERS, C, C), C ** -0.5, 0.375, ((0, 4),)),
    }


def shifted(field, dilation):
    padding = jnp.zeros((dilation, field.shape[1]), field.dtype)
    earlier = jnp.concatenate([padding, field[:-dilation]], axis=0)
    following = jnp.concatenate([field[dilation:], padding], axis=0)
    return (earlier, following)

def layer_forward(hidden, conv_mat, out_mat, dilation):
    earlier, following = shifted(hidden, dilation)
    preact = jnp.dot(earlier, conv_mat[0], preferred_element_type=jnp.float32)
    preact = preact + jnp.dot(hidden, conv_mat[1], preferred_element_type=jnp.float32)
    preact = preact + jnp.dot(following, conv_mat[2], preferred_element_type=jnp.float32)
    chans = hidden.shape[1]
    gated = (jnp.tanh(preact[:, :chans]) * jax.nn.sigmoid(preact[:, chans:])).astype(jnp.bfloat16)
    output = (hidden.astype(jnp.float32) + jnp.dot(gated, out_mat, preferred_element_type=jnp.float32)).astype(jnp.bfloat16)
    return (output, (earlier, hidden, following, preact, gated))

def layer_backward(flowing, stored, conv_mat, out_mat, dilation):
    earlier, hidden, following, preact, gated = stored
    chans = hidden.shape[1]
    grad_half = flowing.astype(jnp.bfloat16)
    out_term = jnp.dot(gated.T, grad_half, preferred_element_type=jnp.float32)
    grad_gated = jnp.dot(grad_half, out_mat.T, preferred_element_type=jnp.float32)
    tanh_part = jnp.tanh(preact[:, :chans])
    sig_part = jax.nn.sigmoid(preact[:, chans:])
    grad_pre = jnp.concatenate([grad_gated * (1.0 - tanh_part * tanh_part) * sig_part, grad_gated * tanh_part * sig_part * (1.0 - sig_part)], axis=1).astype(jnp.bfloat16)
    conv_term = jnp.stack([jnp.dot(earlier.T, grad_pre, preferred_element_type=jnp.float32), jnp.dot(hidden.T, grad_pre, preferred_element_type=jnp.float32), jnp.dot(following.T, grad_pre, preferred_element_type=jnp.float32)])
    grad_first = jnp.dot(grad_pre, conv_mat[0].T, preferred_element_type=jnp.float32).astype(jnp.bfloat16)
    grad_third = jnp.dot(grad_pre, conv_mat[2].T, preferred_element_type=jnp.float32).astype(jnp.bfloat16)
    grad_first = lax.optimization_barrier(grad_first)
    grad_third = lax.optimization_barrier(grad_third)
    unused_low, first_following = shifted(grad_first, dilation)
    third_earlier, unused_high = shifted(grad_third, dilation)
    grad_conv = jnp.dot(grad_pre, conv_mat[1].T, preferred_element_type=jnp.float32)
    grad_conv = grad_conv + first_following.astype(jnp.float32) + third_earlier.astype(jnp.float32)
    return (flowing + grad_conv, conv_term, out_term)

def reference(section_inputs, cotangent, conv_weight, out_weight):
    dilations = [NEAR, FAR]
    grad_scale = 1.0 / math.sqrt(MICRO * WINDOW)
    carried = [cotangent[batch_index].astype(jnp.float32) for batch_index in range(MICRO)]
    input_rows = [None] * SECTIONS
    conv_rows = [None] * SECTIONS
    out_rows = [None] * SECTIONS
    for section_index in reversed(range(SECTIONS)):
        conv_total = jnp.zeros((LAYERS, 3, C, 2 * C), jnp.float32)
        out_total = jnp.zeros((LAYERS, C, C), jnp.float32)
        per_batch = []
        for batch_index in range(MICRO):
            hidden = section_inputs[section_index, batch_index]
            stored = []
            for layer in range(LAYERS):
                hidden, saved = layer_forward(hidden, conv_weight[section_index, layer], out_weight[section_index, layer], dilations[layer])
                stored.append(saved)
            flowing = carried[batch_index]
            conv_parts = [None] * LAYERS
            out_parts = [None] * LAYERS
            for layer in reversed(range(LAYERS)):
                flowing, conv_parts[layer], out_parts[layer] = layer_backward(flowing, stored[layer], conv_weight[section_index, layer], out_weight[section_index, layer], dilations[layer])
            conv_total = conv_total + jnp.stack(conv_parts)
            out_total = out_total + jnp.stack(out_parts)
            per_batch.append(flowing)
            carried[batch_index] = lax.optimization_barrier(flowing.astype(jnp.bfloat16)).astype(jnp.float32)
        input_rows[section_index] = jnp.stack(per_batch)
        conv_rows[section_index] = (conv_total * grad_scale).reshape(LAYERS, 3 * C, 2 * C)
        out_rows[section_index] = out_total * grad_scale
    return (jnp.stack(input_rows), jnp.stack(conv_rows), jnp.stack(out_rows))
```

```python
import functools
import math

import jax
import jax.numpy as jnp
from jax import lax
from jax.experimental import pallas as pl
from jax.experimental.pallas import tpu as pltpu
from jax.sharding import PartitionSpec as P

NEAR = 128
FAR = 1024
CHUNK = 256
MESH = pl.DeviceIdType.MESH
F32 = jnp.float32
BF16 = jnp.bfloat16


def dot_nn(a, b):
    return lax.dot_general(a, b, (((1,), (0,)), ((), ())), preferred_element_type=F32)


def dot_nt(a, b):
    return lax.dot_general(a, b, (((1,), (1,)), ((), ())), preferred_element_type=F32)


def dot_tn(a, b):
    return lax.dot_general(a, b, (((0,), (0,)), ((), ())), preferred_element_type=F32)


def kernel(n, sections, scale, x_ref, cot_ref, cw_ref, ow_ref, ig_ref, cg_ref, og_ref,
           xe, he, fac, gated, gp, gh0, gin, acc, f1s, t1s, f1r, t1r, f0e, t0e, sbuf,
           ct, ot, csend, osend, cpeer, opeer, cpair, opair, crecv, orecv, ssem, rsem):
    micro, rows, chans = x_ref.shape
    depth = cw_ref.shape[0]
    hops = FAR // rows
    near = NEAR
    chips = n // 2
    r = lax.axis_index("seq")
    s = lax.axis_index("section")
    core = lax.rem(r, 2)
    chip = lax.div(r, 2)
    crow, orow = cg_ref.shape[1], og_ref.shape[1]

    counter = [0]
    pending = []

    def make(src, dst, dev, can_send, can_recv):
        i = counter[0]
        counter[0] += 1
        desc = pltpu.make_async_remote_copy(
            src_ref=src, dst_ref=dst, send_sem=ssem.at[i], recv_sem=rsem.at[i],
            device_id=dev, device_id_type=MESH)
        return desc, can_send, can_recv

    def start(item):
        desc, can_send, _ = item
        pending.append(item)
        if can_send is True:
            desc.start()
        else:
            @pl.when(can_send)
            def _():
                desc.start()

    def arrive(item):
        desc, _, can_recv = item
        if can_recv is True:
            desc.wait_recv()
        else:
            @pl.when(can_recv)
            def _():
                desc.wait_recv()

    def at_seq(step):
        return {"seq": lax.rem(r + n + step, n)}

    near_up, near_dn = r < n - 1, r > 0
    far_up, far_dn = r < n - hops, r >= hops
    below = {"section": lax.rem(s + sections - 1, sections)}

    for m in range(micro):
        xe[m, near:near + rows] = x_ref[m]

    @pl.when(s == sections - 1)
    def _():
        gin[...] = cot_ref[...]

    zero = jnp.zeros((near, chans), BF16)
    zrows = jnp.zeros((rows, chans), BF16)

    @pl.when(r == 0)
    def _():
        for m in range(micro):
            xe[m, 0:near] = zero
            t0e[m, 0:near] = zero

    @pl.when(r == n - 1)
    def _():
        for m in range(micro):
            xe[m, near + rows:2 * near + rows] = zero
            f0e[m, rows:rows + near] = zero

    @pl.when(r < hops)
    def _():
        for m in range(micro):
            he[m, 0] = zrows
            t1r[m] = zrows

    @pl.when(r >= n - hops)
    def _():
        for m in range(micro):
            he[m, 2] = zrows
            f1r[m] = zrows

    barrier = pltpu.get_barrier_semaphore()

    def greet(step, carry):
        pl.semaphore_signal(barrier, inc=1, device_id={"seq": lax.rem(r + step, n)},
                            device_id_type=MESH)
        return carry

    lax.fori_loop(1, n, greet, 0)

    @pl.when(s > 0)
    def _():
        pl.semaphore_signal(barrier, inc=1, device_id={"section": s - 1}, device_id_type=MESH)

    @pl.when(s < sections - 1)
    def _():
        pl.semaphore_signal(barrier, inc=1, device_id={"section": s + 1}, device_id_type=MESH)

    at_end = (s == 0) | (s == sections - 1)

    @pl.when(at_end)
    def _():
        pl.semaphore_wait(barrier, n)

    @pl.when(jnp.logical_not(at_end))
    def _():
        pl.semaphore_wait(barrier, n + 1)

    halo = []
    for m in range(micro):
        up = make(xe.at[m, rows:rows + near], xe.at[m, 0:near], at_seq(1), near_up, near_dn)
        dn = make(xe.at[m, near:2 * near], xe.at[m, near + rows:2 * near + rows],
                  at_seq(-1), near_dn, near_up)
        start(up)
        start(dn)
        halo.append((up, dn))

    count = rows // CHUNK
    order = [0, count - 1] + list(range(1, count - 1)) if count > 1 else [0]
    far_h = {}

    def gate(l, m, a, parts):
        pre = dot_nn(parts[0], cw_ref[l, 0])
        pre = pre + dot_nn(parts[1], cw_ref[l, 1])
        pre = pre + dot_nn(parts[2], cw_ref[l, 2])
        t = jnp.tanh(pre[:, :chans])
        sg = 0.5 * jnp.tanh(0.5 * pre[:, chans:]) + 0.5
        ts = t * sg
        fac[l, m, 0, a:a + CHUNK] = (1.0 - t * t) * sg
        fac[l, m, 1, a:a + CHUNK] = ts * (1.0 - sg)
        out = ts.astype(BF16)
        gated[l, m, a:a + CHUNK] = out
        return out

    def forward_near(m):
        for item in halo[m]:
            arrive(item)
        for c in order:
            a = c * CHUNK
            parts = [xe[m, a + k * near:a + k * near + CHUNK] for k in range(3)]
            out = gate(0, m, a, parts)
            nxt = (parts[1].astype(F32) + dot_nn(out, ow_ref[0])).astype(BF16)
            he[m, 1, a:a + CHUNK] = nxt
            up = make(he.at[m, 1, a:a + CHUNK], he.at[m, 0, a:a + CHUNK],
                      at_seq(hops), far_up, far_dn)
            dn = make(he.at[m, 1, a:a + CHUNK], he.at[m, 2, a:a + CHUNK],
                      at_seq(-hops), far_dn, far_up)
            start(up)
            start(dn)
            far_h[m, c] = (up, dn)

    def forward_far(m):
        for c in order:
            a = c * CHUNK
            for item in far_h[m, c]:
                arrive(item)
            gate(1, m, a, [he[m, k, a:a + CHUNK] for k in range(3)])

    relay, far_g, near_g = {}, {}, {}
    for m in range(micro):
        for c in order:
            a = c * CHUNK
            relay[m, c] = make(sbuf.at[m, a:a + CHUNK], gin.at[m, a:a + CHUNK], below,
                               s > 0, s < sections - 1)

    def pre_grad(l, m, a, half):
        gg = dot_nt(half, ow_ref[l])
        gp[l, m, a:a + CHUNK, :chans] = (gg * fac[l, m, 0, a:a + CHUNK]).astype(BF16)
        gp[l, m, a:a + CHUNK, chans:] = (gg * fac[l, m, 1, a:a + CHUNK]).astype(BF16)
        return gp[l, m, a:a + CHUNK]

    def back_far(m, c):
        a = c * CHUNK
        arrive(relay[m, c])
        half = gin[m, a:a + CHUNK]
        grad = pre_grad(1, m, a, half)
        f1s[m, a:a + CHUNK] = dot_nt(grad, cw_ref[1, 0]).astype(BF16)
        dn = make(f1s.at[m, a:a + CHUNK], f1r.at[m, a:a + CHUNK], at_seq(-hops), far_dn, far_up)
        start(dn)
        t1s[m, a:a + CHUNK] = dot_nt(grad, cw_ref[1, 2]).astype(BF16)
        up = make(t1s.at[m, a:a + CHUNK], t1r.at[m, a:a + CHUNK], at_seq(hops), far_up, far_dn)
        start(up)
        far_g[m, c] = (dn, up)
        acc[m, a:a + CHUNK] = half.astype(F32) + dot_nt(grad, cw_ref[1, 1])

    def back_near(m, c):
        a = c * CHUNK
        for item in far_g[m, c]:
            arrive(item)
        flow = acc[m, a:a + CHUNK] + (f1r[m, a:a + CHUNK].astype(F32)
                                      + t1r[m, a:a + CHUNK].astype(F32))
        half = flow.astype(BF16)
        gh0[m, a:a + CHUNK] = half
        grad = pre_grad(0, m, a, half)
        f0e[m, a:a + CHUNK] = dot_nt(grad, cw_ref[0, 0]).astype(BF16)
        if c == 0:
            near_g[m, "hi"] = make(f0e.at[m, 0:near], f0e.at[m, rows:rows + near], at_seq(-1),
                                   near_dn, near_up)
            start(near_g[m, "hi"])
        t0e[m, near + a:near + a + CHUNK] = dot_nt(grad, cw_ref[0, 2]).astype(BF16)
        if c == count - 1:
            near_g[m, "lo"] = make(t0e.at[m, rows:rows + near], t0e.at[m, 0:near], at_seq(1),
                                   near_up, near_dn)
            start(near_g[m, "lo"])
        acc[m, a:a + CHUNK] = flow + dot_nt(grad, cw_ref[0, 1])

    def finish(m, c):
        a = c * CHUNK
        if c == 0:
            arrive(near_g[m, "lo"])
        if c == count - 1:
            arrive(near_g[m, "hi"])
        flow = acc[m, a:a + CHUNK] + (f0e[m, a + near:a + near + CHUNK].astype(F32)
                                      + t0e[m, a:a + CHUNK].astype(F32))
        sbuf[m, a:a + CHUNK] = flow.astype(BF16)
        start(relay[m, c])
        ig_ref[m, a:a + CHUNK] = flow

    def back_near_all(m, between=None):
        done, sent = set(), set()
        for c in order:
            if between is not None:
                between(c)
            back_near(m, c)
            done.add(c)
            for e in order:
                needs = {k for k in (e - 1, e, e + 1) if 0 <= k < count}
                if e not in sent and needs <= done:
                    finish(m, e)
                    sent.add(e)

    def weight_grads(l):
        def tap(k, carry):
            total = None
            for m in range(micro):
                if l == 0:
                    src = xe[m, pl.ds(pl.multiple_of(k * near, near), rows)]
                else:
                    src = he[m, k]
                term = dot_tn(src, gp[l, m])
                total = term if total is None else total + term
            ct[l, pl.ds(pl.multiple_of(k * chans, chans), chans)] = total
            return carry

        lax.fori_loop(0, 3, tap, 0)
        total = None
        for m in range(micro):
            half = gin[m] if l == depth - 1 else gh0[m]
            term = dot_tn(gated[l, m], half)
            total = term if total is None else total + term
        ot[l] = total

    def shard(ref, l, j, size):
        return ref[l, pl.ds(pl.multiple_of(j * size, 8), size)]

    def pair_start(l):
        for i in range(chips):
            j = 2 * i + (1 - core)
            csend[l, i] = shard(ct, l, j, crow).astype(BF16)
            osend[l, i] = shard(ot, l, j, orow).astype(BF16)
        peer = {"seq": r + 1 - 2 * core}
        items = (make(csend.at[l], cpeer.at[l], peer, True, True),
                 make(osend.at[l], opeer.at[l], peer, True, True))
        for item in items:
            start(item)
        return items

    def spread_start(l, items):
        for item in items:
            arrive(item)
        for i in range(chips):
            j = 2 * i + core
            cpair[l, i] = (shard(ct, l, j, crow) + cpeer[l, i].astype(F32)).astype(BF16)
            opair[l, i] = (shard(ot, l, j, orow) + opeer[l, i].astype(F32)).astype(BF16)
        out = []
        for o in range(1, chips):
            other = lax.rem(chip + o, chips)
            dev = {"seq": 2 * other + core}
            pair = (make(cpair.at[l, other], crecv.at[l, o - 1], dev, True, True),
                    make(opair.at[l, other], orecv.at[l, o - 1], dev, True, True))
            for item in pair:
                start(item)
            out.append(pair)
        return out

    def total_up(l, items):
        csum = shard(ct, l, r, crow) + cpeer[l, chip].astype(F32)
        osum = shard(ot, l, r, orow) + opeer[l, chip].astype(F32)
        for o, pair in enumerate(items):
            for item in pair:
                arrive(item)
            csum = csum + crecv[l, o].astype(F32)
            osum = osum + orecv[l, o].astype(F32)
        cg_ref[l] = csum * scale
        og_ref[l] = osum * scale

    for m in range(micro):
        forward_near(m)
    forward_far(0)
    for c in order:
        back_far(0, c)
    for m in range(micro):
        if m + 1 < micro:
            forward_far(m + 1)
            back_near_all(m, functools.partial(back_far, m + 1))
        else:
            back_near_all(m)
    last = depth - 1
    weight_grads(last)
    first_pair = pair_start(last)
    weight_grads(0)
    spread_last = spread_start(last, first_pair)
    second_pair = pair_start(0)
    spread_first = spread_start(0, second_pair)
    total_up(last, spread_last)
    total_up(0, spread_first)
    for desc, can_send, _ in pending:
        if can_send is True:
            desc.wait_send()
        else:
            @pl.when(can_send)
            def _(desc=desc):
                desc.wait_send()


def shards(section_inputs, cotangent, conv_weight, out_weight):
    n = lax.axis_size("seq")
    sections = lax.axis_size("section")
    micro, rows, chans = cotangent.shape
    depth = conv_weight.shape[1]
    scale = 1.0 / math.sqrt(micro * rows * n)
    chips = n // 2
    crow, orow = 3 * chans // n, chans // n
    count = rows // CHUNK
    sems = micro * (2 + 2 * count + 2 * count + 2 + count) + depth * (2 + 2 * (chips - 1))
    plane = lambda *d: pltpu.VMEM((*d, rows, chans), BF16)
    scratch = [
        pltpu.VMEM((micro, rows + 2 * NEAR, chans), BF16),
        plane(micro, 3),
        pltpu.VMEM((depth, micro, 2, rows, chans), F32),
        plane(depth, micro),
        pltpu.VMEM((depth, micro, rows, 2 * chans), BF16),
        plane(micro),
        plane(micro),
        pltpu.VMEM((micro, rows, chans), F32),
        plane(micro), plane(micro), plane(micro), plane(micro),
        pltpu.VMEM((micro, rows + NEAR, chans), BF16),
        pltpu.VMEM((micro, rows + NEAR, chans), BF16),
        plane(micro),
        pltpu.VMEM((depth, 3 * chans, 2 * chans), F32),
        pltpu.VMEM((depth, chans, chans), F32),
    ]
    for lead in (chips, chips, chips, chips - 1):
        scratch.append(pltpu.VMEM((depth, lead, crow, 2 * chans), BF16))
        scratch.append(pltpu.VMEM((depth, lead, orow, chans), BF16))
    scratch += [pltpu.SemaphoreType.DMA((sems,)), pltpu.SemaphoreType.DMA((sems,))]
    ig, cg, og = pl.pallas_call(
        functools.partial(kernel, n, sections, scale),
        out_shape=(
            jax.ShapeDtypeStruct((micro, rows, chans), F32),
            jax.ShapeDtypeStruct((depth, crow, 2 * chans), F32),
            jax.ShapeDtypeStruct((depth, orow, chans), F32),
        ),
        in_specs=[pl.BlockSpec(memory_space=pltpu.VMEM)] * 4,
        out_specs=(pl.BlockSpec(memory_space=pltpu.VMEM),) * 3,
        scratch_shapes=scratch,
        compiler_params=pltpu.CompilerParams(
            collective_id=0, has_side_effects=True, vmem_limit_bytes=56 * 2**20
        ),
    )(section_inputs[0], cotangent, conv_weight[0], out_weight[0])
    return ig[None], cg[None], og[None]


def solution(mesh):
    return jax.shard_map(
        shards,
        mesh=mesh,
        in_specs=(
            P("section", None, "seq", None),
            P(None, "seq", None),
            P("section", None, None, None, None),
            P("section", None, None, None),
        ),
        out_specs=(
            P("section", None, "seq", None),
            P("section", None, "seq", None),
            P("section", None, "seq", None),
        ),
        check_vma=False,
    )
```

```python
import functools
import math

import jax
import jax.numpy as jnp
from jax import lax
from jax.experimental import pallas as pl
from jax.experimental.pallas import tpu as pltpu
from jax.sharding import PartitionSpec as P

NEAR = 128
FAR = 1024
CHUNK = 128
MESH = pl.DeviceIdType.MESH
F32 = jnp.float32
BF16 = jnp.bfloat16


def dot_nn(a, b):
    return lax.dot_general(a, b, (((1,), (0,)), ((), ())), preferred_element_type=F32)


def dot_tn(a, b):
    return lax.dot_general(a, b, (((0,), (0,)), ((), ())), preferred_element_type=F32)


def kernel(n, sections, scale, x_ref, cot_ref, cw_ref, ow_ref, ig_ref, cg_ref, og_ref,
           xe, he, fac, gated, gp, gh0, gin, acc, f1s, t1s, f1r, t1r, f0e, t0e, sbuf,
           ct, ot, csend, osend, cpeer, opeer, cpair, opair, crecv, orecv, cwt, owt, ssem, rsem):
    micro, rows, chans = x_ref.shape
    depth = cw_ref.shape[0]
    hops = FAR // rows
    near = NEAR
    chips = n // 2
    r = lax.axis_index("seq")
    s = lax.axis_index("section")
    core = lax.rem(r, 2)
    chip = lax.div(r, 2)
    crow, orow = cg_ref.shape[1], og_ref.shape[1]

    counter = [0]
    pending = []

    def make(src, dst, dev, can_send, can_recv):
        i = counter[0]
        counter[0] += 1
        desc = pltpu.make_async_remote_copy(
            src_ref=src, dst_ref=dst, send_sem=ssem.at[i], recv_sem=rsem.at[i],
            device_id=dev, device_id_type=MESH)
        pending.append((desc, can_send, can_recv))
        return pending[-1]

    def start(item):
        desc, can_send, _ = item
        if can_send is True:
            desc.start()
        else:
            @pl.when(can_send)
            def _():
                desc.start()

    def arrive(item):
        desc, _, can_recv = item
        if can_recv is True:
            desc.wait_recv()
        else:
            @pl.when(can_recv)
            def _():
                desc.wait_recv()

    def at_seq(step):
        return {"seq": lax.rem(r + n + step, n)}

    near_up, near_dn = r < n - 1, r > 0
    far_up, far_dn = r < n - hops, r >= hops
    below = {"section": lax.rem(s + sections - 1, sections)}

    for m in range(micro):
        xe[m, near:near + rows] = x_ref[m]

    @pl.when(s == sections - 1)
    def _():
        gin[...] = cot_ref[...]

    zero = jnp.zeros((near, chans), BF16)
    zrows = jnp.zeros((rows, chans), BF16)

    @pl.when(r == 0)
    def _():
        for m in range(micro):
            xe[m, 0:near] = zero
            t0e[m, 0:near] = zero

    @pl.when(r == n - 1)
    def _():
        for m in range(micro):
            xe[m, near + rows:2 * near + rows] = zero
            f0e[m, rows:rows + near] = zero

    @pl.when(r < hops)
    def _():
        for m in range(micro):
            he[m, 0] = zrows
            t1r[m] = zrows

    @pl.when(r >= n - hops)
    def _():
        for m in range(micro):
            he[m, 2] = zrows
            f1r[m] = zrows

    barrier = pltpu.get_barrier_semaphore()

    def greet(step, carry):
        pl.semaphore_signal(barrier, inc=1, device_id={"seq": lax.rem(r + step, n)},
                            device_id_type=MESH)
        return carry

    lax.fori_loop(1, n, greet, 0)

    @pl.when(s > 0)
    def _():
        pl.semaphore_signal(barrier, inc=1, device_id={"section": s - 1}, device_id_type=MESH)

    @pl.when(s < sections - 1)
    def _():
        pl.semaphore_signal(barrier, inc=1, device_id={"section": s + 1}, device_id_type=MESH)

    at_end = (s == 0) | (s == sections - 1)

    @pl.when(at_end)
    def _():
        pl.semaphore_wait(barrier, n)

    @pl.when(jnp.logical_not(at_end))
    def _():
        pl.semaphore_wait(barrier, n + 1)

    halo = []
    for m in range(micro):
        up = make(xe.at[m, rows:rows + near], xe.at[m, 0:near], at_seq(1), near_up, near_dn)
        dn = make(xe.at[m, near:2 * near], xe.at[m, near + rows:2 * near + rows],
                  at_seq(-1), near_dn, near_up)
        start(up)
        start(dn)
        halo.append((up, dn))

    for l in range(depth):
        owt[l] = ow_ref[l].T
        for k in range(3):
            cwt[l, k] = cw_ref[l, k].T

    count = rows // CHUNK
    order = [0, count - 1] + list(range(1, count - 1)) if count > 1 else [0]
    far_h = {}

    def gate(l, m, a, parts):
        pre = dot_nn(parts[0], cw_ref[l, 0])
        pre = pre + dot_nn(parts[1], cw_ref[l, 1])
        pre = pre + dot_nn(parts[2], cw_ref[l, 2])
        t = jnp.tanh(pre[:, :chans])
        sg = 0.5 * jnp.tanh(0.5 * pre[:, chans:]) + 0.5
        ts = t * sg
        fac[l, m, 0, a:a + CHUNK] = (1.0 - t * t) * sg
        fac[l, m, 1, a:a + CHUNK] = ts * (1.0 - sg)
        out = ts.astype(BF16)
        gated[l, m, a:a + CHUNK] = out
        return out

    def forward_near(m):
        for item in halo[m]:
            arrive(item)
        for c in order:
            a = c * CHUNK
            parts = [xe[m, a + k * near:a + k * near + CHUNK] for k in range(3)]
            out = gate(0, m, a, parts)
            nxt = (parts[1].astype(F32) + dot_nn(out, ow_ref[0])).astype(BF16)
            he[m, 1, a:a + CHUNK] = nxt
            for item in far_h[m, c]:
                start(item)

    def forward_far(m):
        for c in order:
            a = c * CHUNK
            for item in far_h[m, c]:
                arrive(item)
            gate(1, m, a, [he[m, k, a:a + CHUNK] for k in range(3)])

    relay, far_g, near_g = {}, {}, {}
    for m in range(micro):
        near_g[m, "hi"] = make(f0e.at[m, 0:near], f0e.at[m, rows:rows + near], at_seq(-1),
                               near_dn, near_up)
        near_g[m, "lo"] = make(t0e.at[m, rows:rows + near], t0e.at[m, 0:near], at_seq(1),
                               near_up, near_dn)
        for c in order:
            a = c * CHUNK
            far_h[m, c] = (
                make(he.at[m, 1, a:a + CHUNK], he.at[m, 0, a:a + CHUNK],
                     at_seq(hops), far_up, far_dn),
                make(he.at[m, 1, a:a + CHUNK], he.at[m, 2, a:a + CHUNK],
                     at_seq(-hops), far_dn, far_up))
            far_g[m, c] = (
                make(f1s.at[m, a:a + CHUNK], f1r.at[m, a:a + CHUNK],
                     at_seq(-hops), far_dn, far_up),
                make(t1s.at[m, a:a + CHUNK], t1r.at[m, a:a + CHUNK],
                     at_seq(hops), far_up, far_dn))
    for m in range(micro):
        for c in order:
            a = c * CHUNK
            relay[m, c] = make(sbuf.at[m, a:a + CHUNK], gin.at[m, a:a + CHUNK], below,
                               s > 0, s < sections - 1)

    def pre_grad(l, m, a, half):
        gg = dot_nn(half, owt[l])
        gp[l, m, a:a + CHUNK, :chans] = (gg * fac[l, m, 0, a:a + CHUNK]).astype(BF16)
        gp[l, m, a:a + CHUNK, chans:] = (gg * fac[l, m, 1, a:a + CHUNK]).astype(BF16)
        return gp[l, m, a:a + CHUNK]

    def back_far(m, c):
        a = c * CHUNK
        arrive(relay[m, c])
        half = gin[m, a:a + CHUNK]
        grad = pre_grad(1, m, a, half)
        f1s[m, a:a + CHUNK] = dot_nn(grad, cwt[1, 0]).astype(BF16)
        start(far_g[m, c][0])
        t1s[m, a:a + CHUNK] = dot_nn(grad, cwt[1, 2]).astype(BF16)
        start(far_g[m, c][1])
        acc[m, a:a + CHUNK] = half.astype(F32) + dot_nn(grad, cwt[1, 1])

    def back_near(m, c):
        a = c * CHUNK
        for item in far_g[m, c]:
            arrive(item)
        flow = acc[m, a:a + CHUNK] + (f1r[m, a:a + CHUNK].astype(F32)
                                      + t1r[m, a:a + CHUNK].astype(F32))
        half = flow.astype(BF16)
        gh0[m, a:a + CHUNK] = half
        grad = pre_grad(0, m, a, half)
        f0e[m, a:a + CHUNK] = dot_nn(grad, cwt[0, 0]).astype(BF16)
        if c == 0:
            start(near_g[m, "hi"])
        t0e[m, near + a:near + a + CHUNK] = dot_nn(grad, cwt[0, 2]).astype(BF16)
        if c == count - 1:
            start(near_g[m, "lo"])
        acc[m, a:a + CHUNK] = flow + dot_nn(grad, cwt[0, 1])

    def finish(m, c):
        a = c * CHUNK
        if c == 0:
            arrive(near_g[m, "lo"])
        if c == count - 1:
            arrive(near_g[m, "hi"])
        flow = acc[m, a:a + CHUNK] + (f0e[m, a + near:a + near + CHUNK].astype(F32)
                                      + t0e[m, a:a + CHUNK].astype(F32))
        sbuf[m, a:a + CHUNK] = flow.astype(BF16)
        start(relay[m, c])
        ig_ref[m, a:a + CHUNK] = flow

    def back_near_all(m, between=None):
        done, sent = set(), set()
        for c in order:
            if between is not None:
                between(c)
            back_near(m, c)
            done.add(c)
            for e in order:
                needs = {k for k in (e - 1, e, e + 1) if 0 <= k < count}
                if e not in sent and needs <= done:
                    finish(m, e)
                    sent.add(e)

    def weight_grads(l):
        def tap(k, carry):
            total = None
            for m in range(micro):
                if l == 0:
                    src = xe[m, pl.ds(pl.multiple_of(k * near, near), rows)]
                else:
                    src = he[m, k]
                term = dot_tn(src, gp[l, m])
                total = term if total is None else total + term
            ct[l, pl.ds(pl.multiple_of(k * chans, chans), chans)] = total
            return carry

        lax.fori_loop(0, 3, tap, 0)
        total = None
        for m in range(micro):
            half = gin[m] if l == depth - 1 else gh0[m]
            term = dot_tn(gated[l, m], half)
            total = term if total is None else total + term
        ot[l] = total

    def shard(ref, l, j, size):
        return ref[l, pl.ds(pl.multiple_of(j * size, 8), size)]

    peer = {"seq": r + 1 - 2 * core}
    pairs, spread = {}, {}
    for l in range(depth):
        pairs[l] = (make(csend.at[l], cpeer.at[l], peer, True, True),
                    make(osend.at[l], opeer.at[l], peer, True, True))
        spread[l] = []
        for o in range(1, chips):
            other = lax.rem(chip + o, chips)
            dev = {"seq": 2 * other + core}
            spread[l].append((make(cpair.at[l, other], crecv.at[l, o - 1], dev, True, True),
                              make(opair.at[l, other], orecv.at[l, o - 1], dev, True, True)))

    def pair_start(l):
        for i in range(chips):
            j = 2 * i + (1 - core)
            csend[l, i] = shard(ct, l, j, crow).astype(BF16)
            osend[l, i] = shard(ot, l, j, orow).astype(BF16)
        for item in pairs[l]:
            start(item)

    def spread_start(l):
        for item in pairs[l]:
            arrive(item)
        for i in range(chips):
            j = 2 * i + core
            cpair[l, i] = (shard(ct, l, j, crow) + cpeer[l, i].astype(F32)).astype(BF16)
            opair[l, i] = (shard(ot, l, j, orow) + opeer[l, i].astype(F32)).astype(BF16)
        for pair in spread[l]:
            for item in pair:
                start(item)

    def total_up(l, items):
        csum = shard(ct, l, r, crow) + cpeer[l, chip].astype(F32)
        osum = shard(ot, l, r, orow) + opeer[l, chip].astype(F32)
        for o, pair in enumerate(items):
            for item in pair:
                arrive(item)
            csum = csum + crecv[l, o].astype(F32)
            osum = osum + orecv[l, o].astype(F32)
        cg_ref[l] = csum * scale
        og_ref[l] = osum * scale

    top = s == sections - 1
    last, end = depth - 1, micro - 1

    @pl.when(top)
    def _():
        for m in range(micro):
            if m == 0:
                forward_near(0)
            forward_far(m)
            for c in order:
                back_far(m, c)
            if m < end:
                forward_near(m + 1)
                back_near_all(m)

    @pl.when(jnp.logical_not(top))
    def _():
        for m in range(micro):
            forward_near(m)
        for m in range(micro):
            forward_far(m)
        for c in order:
            back_far(0, c)
        for m in range(end):
            back_near_all(m, functools.partial(back_far, m + 1))

    def reduce_last():
        weight_grads(last)
        pair_start(last)
        spread_start(last)

    back_near_all(end)
    reduce_last()
    weight_grads(0)
    pair_start(0)
    spread_start(0)
    total_up(last, spread[last])
    total_up(0, spread[0])
    for desc, can_send, _ in pending:
        if can_send is True:
            desc.wait_send()
        else:
            @pl.when(can_send)
            def _(desc=desc):
                desc.wait_send()


def shards(section_inputs, cotangent, conv_weight, out_weight):
    n = lax.axis_size("seq")
    sections = lax.axis_size("section")
    micro, rows, chans = cotangent.shape
    depth = conv_weight.shape[1]
    scale = 1.0 / math.sqrt(micro * rows * n)
    chips = n // 2
    crow, orow = 3 * chans // n, chans // n
    count = rows // CHUNK
    sems = micro * (2 + 2 * count + 2 * count + 2 + count) + depth * (2 + 2 * (chips - 1))
    plane = lambda *d: pltpu.VMEM((*d, rows, chans), BF16)
    scratch = [
        pltpu.VMEM((micro, rows + 2 * NEAR, chans), BF16),
        plane(micro, 3),
        pltpu.VMEM((depth, micro, 2, rows, chans), F32),
        plane(depth, micro),
        pltpu.VMEM((depth, micro, rows, 2 * chans), BF16),
        plane(micro),
        plane(micro),
        pltpu.VMEM((micro, rows, chans), F32),
        plane(micro), plane(micro), plane(micro), plane(micro),
        pltpu.VMEM((micro, rows + NEAR, chans), BF16),
        pltpu.VMEM((micro, rows + NEAR, chans), BF16),
        plane(micro),
        pltpu.VMEM((depth, 3 * chans, 2 * chans), F32),
        pltpu.VMEM((depth, chans, chans), F32),
    ]
    for lead in (chips, chips, chips, chips - 1):
        scratch.append(pltpu.VMEM((depth, lead, crow, 2 * chans), BF16))
        scratch.append(pltpu.VMEM((depth, lead, orow, chans), BF16))
    scratch += [
        pltpu.VMEM((depth, 3, 2 * chans, chans), BF16),
        pltpu.VMEM((depth, chans, chans), BF16),
    ]
    scratch += [pltpu.SemaphoreType.DMA((sems,)), pltpu.SemaphoreType.DMA((sems,))]
    ig, cg, og = pl.pallas_call(
        functools.partial(kernel, n, sections, scale),
        out_shape=(
            jax.ShapeDtypeStruct((micro, rows, chans), F32),
            jax.ShapeDtypeStruct((depth, crow, 2 * chans), F32),
            jax.ShapeDtypeStruct((depth, orow, chans), F32),
        ),
        in_specs=[pl.BlockSpec(memory_space=pltpu.VMEM)] * 4,
        out_specs=(pl.BlockSpec(memory_space=pltpu.VMEM),) * 3,
        scratch_shapes=scratch,
        compiler_params=pltpu.CompilerParams(
            collective_id=0, has_side_effects=True, vmem_limit_bytes=56 * 2**20
        ),
    )(section_inputs[0], cotangent, conv_weight[0], out_weight[0])
    return ig[None], cg[None], og[None]


def solution(mesh):
    return jax.shard_map(
        shards,
        mesh=mesh,
        in_specs=(
            P("section", None, "seq", None),
            P(None, "seq", None),
            P("section", None, None, None, None),
            P("section", None, None, None),
        ),
        out_specs=(
            P("section", None, "seq", None),
            P("section", None, "seq", None),
            P("section", None, "seq", None),
        ),
        check_vma=False,
    )
```

```python
import functools
import math

import jax
import jax.numpy as jnp
from jax import lax
from jax.experimental import pallas as pl
from jax.experimental.pallas import tpu as pltpu
from jax.sharding import PartitionSpec as P

NEAR = 128
FAR = 1024
CHUNK = 128
MESH = pl.DeviceIdType.MESH
F32 = jnp.float32
BF16 = jnp.bfloat16


def dot_nn(a, b):
    return lax.dot_general(a, b, (((1,), (0,)), ((), ())), preferred_element_type=F32)


def dot_tn(a, b):
    return lax.dot_general(a, b, (((0,), (0,)), ((), ())), preferred_element_type=F32)


def kernel(n, sections, scale, x_ref, cot_ref, cw_ref, ow_ref, ig_ref, cg_ref, og_ref,
           xe, he, fac, gated, gp, gh0, gin, acc, f1s, t1s, f1r, t1r, f0e, t0e, sbuf,
           ct, ot, csend, osend, cpeer, opeer, cpair, opair, crecv, orecv, cwt, owt, ssem, rsem):
    micro, rows, chans = x_ref.shape
    depth = cw_ref.shape[0]
    hops = FAR // rows
    near = NEAR
    chips = n // 2
    r = lax.axis_index("seq")
    s = lax.axis_index("section")
    core = lax.rem(r, 2)
    chip = lax.div(r, 2)
    crow, orow = cg_ref.shape[1], og_ref.shape[1]

    counter = [0]
    pending = []

    def make(src, dst, dev, can_send, can_recv):
        i = counter[0]
        counter[0] += 1
        desc = pltpu.make_async_remote_copy(
            src_ref=src, dst_ref=dst, send_sem=ssem.at[i], recv_sem=rsem.at[i],
            device_id=dev, device_id_type=MESH)
        pending.append((desc, can_send, can_recv))
        return pending[-1]

    def start(item):
        desc, can_send, _ = item
        if can_send is True:
            desc.start()
        else:
            @pl.when(can_send)
            def _():
                desc.start()

    def arrive(item):
        desc, _, can_recv = item
        if can_recv is True:
            desc.wait_recv()
        else:
            @pl.when(can_recv)
            def _():
                desc.wait_recv()

    def at_seq(step):
        return {"seq": lax.rem(r + n + step, n)}

    near_up, near_dn = r < n - 1, r > 0
    far_up, far_dn = r < n - hops, r >= hops
    below = {"section": lax.rem(s + sections - 1, sections)}

    for m in range(micro):
        xe[m, near:near + rows] = x_ref[m]

    @pl.when(s == sections - 1)
    def _():
        gin[...] = cot_ref[...]

    zero = jnp.zeros((near, chans), BF16)
    zrows = jnp.zeros((rows, chans), BF16)

    @pl.when(r == 0)
    def _():
        for m in range(micro):
            xe[m, 0:near] = zero
            t0e[m, 0:near] = zero

    @pl.when(r == n - 1)
    def _():
        for m in range(micro):
            xe[m, near + rows:2 * near + rows] = zero
            f0e[m, rows:rows + near] = zero

    @pl.when(r < hops)
    def _():
        for m in range(micro):
            he[m, 0] = zrows
            t1r[m] = zrows

    @pl.when(r >= n - hops)
    def _():
        for m in range(micro):
            he[m, 2] = zrows
            f1r[m] = zrows

    barrier = pltpu.get_barrier_semaphore()

    def greet(step, carry):
        pl.semaphore_signal(barrier, inc=1, device_id={"seq": lax.rem(r + step, n)},
                            device_id_type=MESH)
        return carry

    lax.fori_loop(1, n, greet, 0)

    @pl.when(s > 0)
    def _():
        pl.semaphore_signal(barrier, inc=1, device_id={"section": s - 1}, device_id_type=MESH)

    @pl.when(s < sections - 1)
    def _():
        pl.semaphore_signal(barrier, inc=1, device_id={"section": s + 1}, device_id_type=MESH)

    at_end = (s == 0) | (s == sections - 1)

    @pl.when(at_end)
    def _():
        pl.semaphore_wait(barrier, n)

    @pl.when(jnp.logical_not(at_end))
    def _():
        pl.semaphore_wait(barrier, n + 1)

    halo = []
    for m in range(micro):
        up = make(xe.at[m, rows:rows + near], xe.at[m, 0:near], at_seq(1), near_up, near_dn)
        dn = make(xe.at[m, near:2 * near], xe.at[m, near + rows:2 * near + rows],
                  at_seq(-1), near_dn, near_up)
        start(up)
        start(dn)
        halo.append((up, dn))

    for l in range(depth):
        owt[l] = ow_ref[l].T
        for k in range(3):
            cwt[l, k] = cw_ref[l, k].T

    count = rows // CHUNK
    order = [0, count - 1] + list(range(1, count - 1)) if count > 1 else [0]
    far_h = {}

    def gate(l, m, a, parts):
        pre = dot_nn(parts[0], cw_ref[l, 0])
        pre = pre + dot_nn(parts[1], cw_ref[l, 1])
        pre = pre + dot_nn(parts[2], cw_ref[l, 2])
        t = jnp.tanh(pre[:, :chans])
        sg = 0.5 * jnp.tanh(0.5 * pre[:, chans:]) + 0.5
        ts = t * sg
        fac[l, m, 0, a:a + CHUNK] = (1.0 - t * t) * sg
        fac[l, m, 1, a:a + CHUNK] = ts * (1.0 - sg)
        out = ts.astype(BF16)
        gated[l, m, a:a + CHUNK] = out
        return out

    def forward_near(m):
        for item in halo[m]:
            arrive(item)
        for c in order:
            a = c * CHUNK
            parts = [xe[m, a + k * near:a + k * near + CHUNK] for k in range(3)]
            out = gate(0, m, a, parts)
            nxt = (parts[1].astype(F32) + dot_nn(out, ow_ref[0])).astype(BF16)
            he[m, 1, a:a + CHUNK] = nxt
            for item in far_h[m, c]:
                start(item)

    def forward_far(m):
        for c in order:
            a = c * CHUNK
            for item in far_h[m, c]:
                arrive(item)
            gate(1, m, a, [he[m, k, a:a + CHUNK] for k in range(3)])

    relay, far_g, near_g = {}, {}, {}
    for m in range(micro):
        near_g[m, "hi"] = make(f0e.at[m, 0:near], f0e.at[m, rows:rows + near], at_seq(-1),
                               near_dn, near_up)
        near_g[m, "lo"] = make(t0e.at[m, rows:rows + near], t0e.at[m, 0:near], at_seq(1),
                               near_up, near_dn)
        for c in order:
            a = c * CHUNK
            far_h[m, c] = (
                make(he.at[m, 1, a:a + CHUNK], he.at[m, 0, a:a + CHUNK],
                     at_seq(hops), far_up, far_dn),
                make(he.at[m, 1, a:a + CHUNK], he.at[m, 2, a:a + CHUNK],
                     at_seq(-hops), far_dn, far_up))
            far_g[m, c] = (
                make(f1s.at[m, a:a + CHUNK], f1r.at[m, a:a + CHUNK],
                     at_seq(-hops), far_dn, far_up),
                make(t1s.at[m, a:a + CHUNK], t1r.at[m, a:a + CHUNK],
                     at_seq(hops), far_up, far_dn))
    for m in range(micro):
        for c in order:
            a = c * CHUNK
            relay[m, c] = make(sbuf.at[m, a:a + CHUNK], gin.at[m, a:a + CHUNK], below,
                               s > 0, s < sections - 1)

    def pre_grad(l, m, a, half):
        gg = dot_nn(half, owt[l])
        gp[l, m, a:a + CHUNK, :chans] = (gg * fac[l, m, 0, a:a + CHUNK]).astype(BF16)
        gp[l, m, a:a + CHUNK, chans:] = (gg * fac[l, m, 1, a:a + CHUNK]).astype(BF16)
        return gp[l, m, a:a + CHUNK]

    def back_far(m, c):
        a = c * CHUNK
        arrive(relay[m, c])
        half = gin[m, a:a + CHUNK]
        grad = pre_grad(1, m, a, half)
        f1s[m, a:a + CHUNK] = dot_nn(grad, cwt[1, 0]).astype(BF16)
        start(far_g[m, c][0])
        t1s[m, a:a + CHUNK] = dot_nn(grad, cwt[1, 2]).astype(BF16)
        start(far_g[m, c][1])
        acc[m, a:a + CHUNK] = half.astype(F32) + dot_nn(grad, cwt[1, 1])

    def back_near(m, c):
        a = c * CHUNK
        for item in far_g[m, c]:
            arrive(item)
        flow = acc[m, a:a + CHUNK] + (f1r[m, a:a + CHUNK].astype(F32)
                                      + t1r[m, a:a + CHUNK].astype(F32))
        half = flow.astype(BF16)
        gh0[m, a:a + CHUNK] = half
        grad = pre_grad(0, m, a, half)
        f0e[m, a:a + CHUNK] = dot_nn(grad, cwt[0, 0]).astype(BF16)
        if c == 0:
            start(near_g[m, "hi"])
        t0e[m, near + a:near + a + CHUNK] = dot_nn(grad, cwt[0, 2]).astype(BF16)
        if c == count - 1:
            start(near_g[m, "lo"])
        acc[m, a:a + CHUNK] = flow + dot_nn(grad, cwt[0, 1])

    def finish(m, c):
        a = c * CHUNK
        if c == 0:
            arrive(near_g[m, "lo"])
        if c == count - 1:
            arrive(near_g[m, "hi"])
        flow = acc[m, a:a + CHUNK] + (f0e[m, a + near:a + near + CHUNK].astype(F32)
                                      + t0e[m, a:a + CHUNK].astype(F32))
        sbuf[m, a:a + CHUNK] = flow.astype(BF16)
        start(relay[m, c])
        ig_ref[m, a:a + CHUNK] = flow

    def back_near_all(m, between=None):
        done, sent = set(), set()
        for c in order:
            if between is not None:
                between(c)
            back_near(m, c)
            done.add(c)
            for e in order:
                needs = {k for k in (e - 1, e, e + 1) if 0 <= k < count}
                if e not in sent and needs <= done:
                    finish(m, e)
                    sent.add(e)

    def weight_grads(l):
        def tap(k, carry):
            total = None
            for m in range(micro):
                if l == 0:
                    src = xe[m, pl.ds(pl.multiple_of(k * near, near), rows)]
                else:
                    src = he[m, k]
                term = dot_tn(src, gp[l, m])
                total = term if total is None else total + term
            ct[l, pl.ds(pl.multiple_of(k * chans, chans), chans)] = total
            return carry

        lax.fori_loop(0, 3, tap, 0)
        total = None
        for m in range(micro):
            half = gin[m] if l == depth - 1 else gh0[m]
            term = dot_tn(gated[l, m], half)
            total = term if total is None else total + term
        ot[l] = total

    def shard(ref, l, j, size):
        return ref[l, pl.ds(pl.multiple_of(j * size, 8), size)]

    peer = {"seq": r + 1 - 2 * core}
    pairs, spread = {}, {}
    for l in range(depth):
        pairs[l] = (make(csend.at[l], cpeer.at[l], peer, True, True),
                    make(osend.at[l], opeer.at[l], peer, True, True))
        spread[l] = []
        for o in range(1, chips):
            other = lax.rem(chip + o, chips)
            dev = {"seq": 2 * other + core}
            spread[l].append((make(cpair.at[l, other], crecv.at[l, o - 1], dev, True, True),
                              make(opair.at[l, other], orecv.at[l, o - 1], dev, True, True)))

    def pair_start(l):
        for i in range(chips):
            j = 2 * i + (1 - core)
            csend[l, i] = shard(ct, l, j, crow).astype(BF16)
            osend[l, i] = shard(ot, l, j, orow).astype(BF16)
        for item in pairs[l]:
            start(item)

    def spread_start(l):
        for item in pairs[l]:
            arrive(item)
        for i in range(chips):
            j = 2 * i + core
            cpair[l, i] = (shard(ct, l, j, crow) + cpeer[l, i].astype(F32)).astype(BF16)
            opair[l, i] = (shard(ot, l, j, orow) + opeer[l, i].astype(F32)).astype(BF16)
        for pair in spread[l]:
            for item in pair:
                start(item)

    def total_up(l, items):
        csum = shard(ct, l, r, crow) + cpeer[l, chip].astype(F32)
        osum = shard(ot, l, r, orow) + opeer[l, chip].astype(F32)
        for o, pair in enumerate(items):
            for item in pair:
                arrive(item)
            csum = csum + crecv[l, o].astype(F32)
            osum = osum + orecv[l, o].astype(F32)
        cg_ref[l] = csum * scale
        og_ref[l] = osum * scale

    top = s == sections - 1
    last, end = depth - 1, micro - 1

    @pl.when(top)
    def _():
        for m in range(micro):
            if m == 0:
                forward_near(0)
            forward_far(m)
            for c in order:
                back_far(m, c)
            if m < end:
                forward_near(m + 1)
                back_near_all(m)

    @pl.when(jnp.logical_not(top))
    def _():
        for m in range(micro):
            forward_near(m)
        for m in range(micro):
            forward_far(m)
        for m in range(micro):
            for c in order:
                back_far(m, c)
            if m < end:
                back_near_all(m)

    def reduce_last():
        weight_grads(last)
        pair_start(last)
        spread_start(last)

    back_near_all(end)
    reduce_last()
    weight_grads(0)
    pair_start(0)
    spread_start(0)
    total_up(last, spread[last])
    total_up(0, spread[0])
    for desc, can_send, _ in pending:
        if can_send is True:
            desc.wait_send()
        else:
            @pl.when(can_send)
            def _(desc=desc):
                desc.wait_send()


def shards(section_inputs, cotangent, conv_weight, out_weight):
    n = lax.axis_size("seq")
    sections = lax.axis_size("section")
    micro, rows, chans = cotangent.shape
    depth = conv_weight.shape[1]
    scale = 1.0 / math.sqrt(micro * rows * n)
    chips = n // 2
    crow, orow = 3 * chans // n, chans // n
    count = rows // CHUNK
    sems = micro * (2 + 2 * count + 2 * count + 2 + count) + depth * (2 + 2 * (chips - 1))
    plane = lambda *d: pltpu.VMEM((*d, rows, chans), BF16)
    scratch = [
        pltpu.VMEM((micro, rows + 2 * NEAR, chans), BF16),
        plane(micro, 3),
        pltpu.VMEM((depth, micro, 2, rows, chans), F32),
        plane(depth, micro),
        pltpu.VMEM((depth, micro, rows, 2 * chans), BF16),
        plane(micro),
        plane(micro),
        pltpu.VMEM((micro, rows, chans), F32),
        plane(micro), plane(micro), plane(micro), plane(micro),
        pltpu.VMEM((micro, rows + NEAR, chans), BF16),
        pltpu.VMEM((micro, rows + NEAR, chans), BF16),
        plane(micro),
        pltpu.VMEM((depth, 3 * chans, 2 * chans), F32),
        pltpu.VMEM((depth, chans, chans), F32),
    ]
    for lead in (chips, chips, chips, chips - 1):
        scratch.append(pltpu.VMEM((depth, lead, crow, 2 * chans), BF16))
        scratch.append(pltpu.VMEM((depth, lead, orow, chans), BF16))
    scratch += [
        pltpu.VMEM((depth, 3, 2 * chans, chans), BF16),
        pltpu.VMEM((depth, chans, chans), BF16),
    ]
    scratch += [pltpu.SemaphoreType.DMA((sems,)), pltpu.SemaphoreType.DMA((sems,))]
    ig, cg, og = pl.pallas_call(
        functools.partial(kernel, n, sections, scale),
        out_shape=(
            jax.ShapeDtypeStruct((micro, rows, chans), F32),
            jax.ShapeDtypeStruct((depth, crow, 2 * chans), F32),
            jax.ShapeDtypeStruct((depth, orow, chans), F32),
        ),
        in_specs=[pl.BlockSpec(memory_space=pltpu.VMEM)] * 4,
        out_specs=(pl.BlockSpec(memory_space=pltpu.VMEM),) * 3,
        scratch_shapes=scratch,
        compiler_params=pltpu.CompilerParams(
            collective_id=0, has_side_effects=True, vmem_limit_bytes=56 * 2**20
        ),
    )(section_inputs[0], cotangent, conv_weight[0], out_weight[0])
    return ig[None], cg[None], og[None]


def solution(mesh):
    return jax.shard_map(
        shards,
        mesh=mesh,
        in_specs=(
            P("section", None, "seq", None),
            P(None, "seq", None),
            P("section", None, None, None, None),
            P("section", None, None, None),
        ),
        out_specs=(
            P("section", None, "seq", None),
            P("section", None, "seq", None),
            P("section", None, "seq", None),
        ),
        check_vma=False,
    )
```
